128 devices in a mesh: ex: 8 (over y_hi, x), ey: 4 (over y_lo, core), dp: 4 (over z).
Axes of the slice: x: 4, y: 4 (y_hi: 2, y_lo: 2; y = y_hi * 2 + y_lo), z: 4, core: 2. Of those that a mesh axis runs over, the one named last changes fastest.
Arguments:
- tokens: bfloat16 [2048, 2048], P(('ex', 'ey', 'dp')), may hold values from -6 to 6
- cotangent: bfloat16 [2048, 2048], P(('ex', 'ey', 'dp')), may hold values from -1.796875 to 1.796875
- route_weights: float32 [2048, 2], P(('ex', 'ey', 'dp')), may hold values from 0.2 to 1
- expert_ids: int32 [2048, 2], P(('ex', 'ey', 'dp')), may hold values from 0 to 15, as said below
- slot_ids: int32 [2048, 2], P(('ex', 'ey', 'dp')), may hold values from -1 to 1, as said below
- gate_weight: bfloat16 [16, 2048, 8192], P('ex', None, ('ey', 'dp')), may hold values from -0.125 to 0.125
- up_weight: bfloat16 [16, 2048, 8192], P('ex', None, ('ey', 'dp')), may hold values from -0.125 to 0.125
- down_weight: bfloat16 [16, 8192, 2048], P('ex', ('ey', 'dp')), may hold values from -0.0625 to 0.0625
Outputs:
- grad_tokens: bfloat16 [2048, 2048], P(('ex', 'ey', 'dp'))
- grad_gate: bfloat16 [16, 2048, 8192], P('ex', None, ('ey', 'dp'))
- grad_up: bfloat16 [16, 2048, 8192], P('ex', None, ('ey', 'dp'))
- grad_down: bfloat16 [16, 8192, 2048], P('ex', ('ey', 'dp'))
The draws below stay inside these ranges and needn't reach their ends.
Inputs may be any that keep to these rules, and one draw needn't show every extreme that they name: `expert_ids`: each token names 2 different experts. `slot_ids`: within the tokens of one device, the choices that name one expert, taken in order of token and then of choice, hold slots 0, 1, 2 and so on; those past 2 of them hold -1. In every draw some expert is given 2 rows by every device.
All inputs are finite; a program needn't handle non-finite values.
Results may differ from the reference program's by a relative error of at most 0.0058.
Values may be sent and summed in bfloat16 or wider, within the bound.
A program may use at most 128 MiB of HBM per device.

```python
import jax
import jax.numpy as jnp
from jax import lax

D = 2048
FF = 8192
TOP = 2
TOK_DEV = 16
EXPERTS = 16
CAP = 2
TOKENS = 2048
DEVICES = 128


def route_table(key):
    subkeys = jax.random.split(key, 4)
    expert_iota = jnp.arange(EXPERTS, dtype=jnp.int32)
    scores = jax.random.randint(subkeys[0], (DEVICES, TOK_DEV, EXPERTS), 0, 1 << 16) * EXPERTS + expert_iota
    favour = jax.random.randint(subkeys[1], (EXPERTS,), 0, 4) * (EXPERTS << 14)
    hottest = jax.random.randint(subkeys[2], (), 0, EXPERTS)
    order_keys = jax.random.randint(subkeys[3], (DEVICES, TOK_DEV), 0, 1 << 16) * TOK_DEV + jnp.arange(TOK_DEV, dtype=jnp.int32)
    token_rank = jnp.sum((order_keys[:, None, :] < order_keys[:, :, None]).astype(jnp.int32), axis=2)
    forced = token_rank <= CAP
    raised = jnp.where(forced[:, :, None] & (expert_iota[None, None, :] == hottest), EXPERTS << 20, 0)
    scores = scores + favour[None, None, :] + raised
    chosen_ids = lax.top_k(scores, TOP)[1].astype(jnp.int32)
    pair_table = (chosen_ids[..., None] == expert_iota).astype(jnp.int32).reshape(DEVICES, TOK_DEV * TOP, EXPERTS)
    running = jnp.cumsum(pair_table, axis=1) - 1
    slot_rank = jnp.sum(running * pair_table, axis=2).reshape(DEVICES, TOK_DEV, TOP)
    slot_table = jnp.where(slot_rank < CAP, slot_rank, -1).astype(jnp.int32)
    return (chosen_ids.reshape(TOKENS, TOP), slot_table.reshape(TOKENS, TOP))


def draw_expert_ids(key, part):
    return route_table(key)[0]


def draw_slot_ids(key, part):
    return route_table(key)[1]


def steps_of(stream_key, extent, shards, low, top_value):
    level, own = 1.0, jax.random.fold_in(stream_key, 6)
    for dim, shards_of in shards:
        draws = jnp.exp(jax.random.uniform(jax.random.fold_in(own, dim), (shards_of,), jnp.float32, low / len(shards), top_value / len(shards)))
        level = level * jnp.repeat(draws, extent[dim] // shards_of).reshape([-1 if axis == dim else 1 for axis in range(len(extent))])
    return level


def scatter_about(own_key, shape, scale, bound, cuts=(), kind=jnp.bfloat16):
    array = scale * jax.random.normal(own_key, shape, jnp.float32)
    if cuts:
        array = array * steps_of(own_key, shape, cuts, -0.22, 0.18)
    return jnp.clip(array, -bound, bound).astype(kind)


def setup_inputs(seed: int = 0) -> dict:
    key_of = jax.random.split(jax.random.key(seed), 9)
    tokens = scatter_about(key_of[0], (TOKENS, D), 1.0, 6.0, ((0, 128),))
    cotangent = scatter_about(key_of[1], (TOKENS, D), 0.3, 1.796875, ((0, 128),))
    route_weights = jnp.clip(0.2 + 0.8 * jax.random.uniform(key_of[2], (TOKENS, TOP), jnp.float32) ** steps_of(key_of[2], (TOKENS, TOP), ((0, 128),), -0.2, 0.2), 0.2, 1.0)
    expert_ids = draw_expert_ids(jax.random.fold_in(key_of[8], 71), 0)
    slot_ids = draw_slot_ids(jax.random.fold_in(key_of[8], 71), 0)
    gate_weight = scatter_about(key_of[5], (EXPERTS, D, FF), D ** -0.5, 0.125, ((0, 8), (2, 16)))
    up_weight = scatter_about(key_of[6], (EXPERTS, D, FF), D ** -0.5, 0.125, ((0, 8), (2, 16)))
    down_weight = scatter_about(key_of[7], (EXPERTS, FF, D), FF ** -0.5, 0.0625, ((0, 8), (1, 16)))
    return {"tokens": tokens, "cotangent": cotangent, "route_weights": route_weights, "expert_ids": expert_ids, "slot_ids": slot_ids, "gate_weight": gate_weight, "up_weight": up_weight, "down_weight": down_weight}


def smooth(argument):
    return jax.nn.gelu(argument, approximate=True)

def expert_backward(inputs, routed, gate_matrix, up_matrix, down_matrix):
    pre_gate = jnp.dot(inputs, gate_matrix, preferred_element_type=jnp.float32)
    pre_up = jnp.dot(inputs, up_matrix, preferred_element_type=jnp.float32)
    activated, backward = jax.vjp(smooth, pre_gate)
    hidden = (activated * pre_up).astype(jnp.bfloat16)
    grad_hidden = jnp.dot(routed, down_matrix.T, preferred_element_type=jnp.float32)
    grad_up_rows = (grad_hidden * activated).astype(jnp.bfloat16)
    grad_gate_rows = backward(grad_hidden * pre_up)[0].astype(jnp.bfloat16)
    gate_grad = jnp.dot(inputs.T, grad_gate_rows, preferred_element_type=jnp.float32).astype(jnp.bfloat16)
    up_grad = jnp.dot(inputs.T, grad_up_rows, preferred_element_type=jnp.float32).astype(jnp.bfloat16)
    down_grad = jnp.dot(hidden.T, routed, preferred_element_type=jnp.float32).astype(jnp.bfloat16)
    expert_grad = jnp.dot(grad_gate_rows, gate_matrix.T, preferred_element_type=jnp.float32)
    expert_grad = expert_grad + jnp.dot(grad_up_rows, up_matrix.T, preferred_element_type=jnp.float32)
    return (gate_grad, up_grad, down_grad, expert_grad)

def reference(tokens, cotangent, route_weights, expert_ids, slot_ids, gate_weight, up_weight, down_weight):
    buffer_rows = DEVICES * CAP
    source = (jnp.arange(TOKENS, dtype=jnp.int32) // TOK_DEV)[:, None]
    is_live = slot_ids >= 0
    position = jnp.where(is_live, source * CAP + slot_ids, buffer_rows).astype(jnp.int32)
    spread_tokens = jnp.broadcast_to(tokens[:, None, :], (TOKENS, TOP, D))
    routed_rows = (route_weights[:, :, None] * cotangent.astype(jnp.float32)[:, None, :]).astype(jnp.bfloat16)
    expert_inputs = jnp.zeros((EXPERTS, buffer_rows, D), jnp.bfloat16).at[expert_ids, position].set(spread_tokens, mode='drop')
    routed_grad = jnp.zeros((EXPERTS, buffer_rows, D), jnp.bfloat16).at[expert_ids, position].set(routed_rows, mode='drop')
    results = lax.map(lambda bundle: expert_backward(*bundle), (expert_inputs, routed_grad, gate_weight, up_weight, down_weight))
    grad_gate, grad_up, grad_down, expert_grad = results
    picked = expert_grad[expert_ids, jnp.minimum(position, buffer_rows - 1)]
    grad_tokens = lax.optimization_barrier(jnp.sum(jnp.where(is_live[:, :, None], picked, 0.0), axis=1)).astype(jnp.bfloat16)
    return (grad_tokens, grad_gate, grad_up, grad_down)
```

```python
import jax
import jax.numpy as jnp
from jax import lax
from jax.experimental import pallas as pl
from jax.experimental.pallas import tpu as pltpu
from jax.sharding import PartitionSpec as P

MESH = pl.DeviceIdType.MESH
F32 = jnp.float32
BF16 = jnp.bfloat16

NX = 4
NZ = 4
PEERS = 8
BLOCKS = 16
TILE = 16


def dot(a, b, ca, cb):
    return lax.dot_general(a, b, (((ca,), (cb,)), ((), ())), preferred_element_type=F32)


def onehot(mask):
    return jnp.where(mask, 1.0, 0.0).astype(BF16)


def block_row(dc, dyl, dz):
    return TILE * (dc * 8 + dyl * 4 + dz)


def main_kernel(
    tok_ref, cot_ref, rw_ref, ids_ref, slots_ref, wg_hbm, wu_hbm, wd_hbm,
    gtok_ref, rows, hid_ref, gg_ref, gu_ref,
    wg, wu, wd, send1, recv1, acc, pair_out, pair_in,
    z2_out, z2_in, zp_out, zp_in, zm_out, zm_in, y0_out, y0_in, y1_out, y1_in,
    ret_out, ret_in, w_sem, send_sem, recv_sem,
):
    ex, ey, dp = lax.axis_index("ex"), lax.axis_index("ey"), lax.axis_index("dp")
    yh, x = ex // NX, ex % NX
    yl, core = ey // 2, ey % 2
    width = tok_ref.shape[1]
    half, quarter = width // 2, width // 4
    hidden = wg.shape[2]

    def peer(k, sign):
        dyh, dx = k // NX, k % NX
        other_yl = (yl + dyh) % 2
        return (((yh + dyh) % 2) * NX + (x + sign * dx + NX) % NX, other_yl * 2 + core, dp)

    z_plus = (ex, ey, (dp + 1) % NZ)
    z_minus = (ex, ey, (dp + NZ - 1) % NZ)
    y_pair = (ex, (1 - yl) * 2 + core, dp)
    sibling = (ex, yl * 2 + (1 - core), dp)

    barrier = pltpu.get_barrier_semaphore()
    partners = [peer(k, 1) for k in range(1, PEERS)] + [z_plus, z_minus, y_pair, sibling]
    for device in partners:
        pl.semaphore_signal(barrier, inc=1, device_id=device, device_id_type=MESH)

    loads = []
    for e in range(2):
        for n, (source, target) in enumerate(((wg_hbm, wg), (wu_hbm, wu), (wd_hbm, wd))):
            copy = pltpu.make_async_copy(source.at[e], target.at[e], w_sem.at[e * 3 + n])
            copy.start()
            loads.append(copy)

    lane = lax.broadcasted_iota(jnp.int32, (16, 128), 1)
    piece = lane // 16
    group = ((yh + piece // NX) % 2) * NX + (x + piece % NX) % NX
    slot_of = lane % 2
    expert_of = group * 2 + (lane // 2) % 2
    ids, slots = ids_ref[...], slots_ref[...]
    match = [
        jnp.where((ids[:, k : k + 1] == expert_of) & (slots[:, k : k + 1] == slot_of), 1.0, 0.0)
        for k in range(2)
    ]
    rw = rw_ref[...]
    cot = cot_ref[...].astype(F32)
    routed = [(rw[:, k : k + 1] * cot).astype(BF16) for k in range(2)]
    stacked = jnp.concatenate([tok_ref[...], routed[0], routed[1]], axis=0)
    is_grad = (lane // 4) % 2 == 1
    pick = jnp.concatenate(
        [
            jnp.where(is_grad, 0.0, match[0] + match[1]),
            jnp.where(is_grad, match[0], 0.0),
            jnp.where(is_grad, match[1], 0.0),
        ],
        axis=0,
    )
    lane48 = lax.broadcasted_iota(jnp.int32, (48, 128), 1)
    upper = (lane48 // 8) % 2 == 1
    built = dot(jnp.where(upper, 0.0, pick).astype(BF16), stacked[:, :half], 0, 0)
    built += dot(jnp.where(upper, pick, 0.0).astype(BF16), stacked[:, half:], 0, 0)
    send1[...] = built.astype(BF16)

    pl.semaphore_wait(barrier, len(partners))

    count = [0, 0]
    sent = []

    def remote(src, dst, device, recv_index):
        index = count[0]
        count[0] += 1
        copy = pltpu.make_async_remote_copy(
            src_ref=src,
            dst_ref=dst,
            send_sem=send_sem.at[index],
            recv_sem=recv_sem.at[recv_index],
            device_id=device,
            device_id_type=MESH,
        )
        copy.start()
        sent.append(copy)
        return copy

    def fresh():
        count[1] += 1
        return count[1] - 1

    first = []
    for k in range(1, PEERS):
        part = pl.ds(k * TILE, TILE)
        first.append(remote(send1.at[part], recv1.at[part], peer(k, 1), fresh()))
    recv1[0:TILE] = send1[0:TILE]
    for copy in first:
        copy.wait_recv()
    row_o = lax.broadcasted_iota(jnp.int32, (64, 128), 0)
    lane_o = lax.broadcasted_iota(jnp.int32, (64, 128), 1)
    wanted = (
        ((row_o % 16) // 2) * 16 + ((row_o // 16) % 2) * 4 + (row_o // 32) * 2 + row_o % 2
    )
    pieces = recv1[...]
    for h in range(2):
        block = dot(onehot(lane_o == wanted + 8 * h), pieces, 1, 0).astype(BF16)
        for s in range(4):
            rows[s, 0:TILE, h * half : (h + 1) * half] = block[s * TILE : (s + 1) * TILE]

    arrive = {}

    def move(s, here, there, device):
        src = rows.at[s, pl.ds(block_row(*here), TILE)]
        dst = rows.at[s, pl.ds(block_row(*there), TILE)]
        arrive[s, there] = remote(src, dst, device, fresh())

    def arrived(s, block):
        arrive[s, block].wait_recv()

    def share(s, dyl):
        src = rows.at[s, pl.ds(block_row(0, dyl, 0), 4 * TILE)]
        dst = rows.at[s, pl.ds(block_row(1, dyl, 0), 4 * TILE)]
        arrive[s, "share", dyl] = remote(src, dst, sibling, fresh())

    def ring(s, dyl):
        move(s, (0, dyl, 0), (0, dyl, 3), z_plus)
        move(s, (0, dyl, 0), (0, dyl, 1), z_minus)

    def onward(s, dyl, up):
        if up:
            move(s, (0, dyl, 3), (0, dyl, 2), z_plus)
        else:
            move(s, (0, dyl, 1), (0, dyl, 2), z_minus)

    for e in range(2):
        xs, gs = 2 * e, 2 * e + 1
        move(xs, (0, 0, 0), (0, 1, 0), y_pair)
        ring(gs, 0)
        ring(xs, 0)
        move(gs, (0, 0, 0), (0, 1, 0), y_pair)
    for e in range(2):
        xs, gs = 2 * e, 2 * e + 1
        up = e == 0
        arrived(xs, (0, 1, 0))
        ring(xs, 1)
        arrived(gs, (0, 0, 3))
        arrived(gs, (0, 0, 1))
        onward(gs, 0, not up)
        move(gs, (0, 0, 3), (0, 1, 3), y_pair)
        move(gs, (0, 0, 1), (0, 1, 1), y_pair)
        arrived(xs, (0, 0, 3))
        arrived(xs, (0, 0, 1))
        onward(xs, 0, up)
    for e in range(2):
        xs, gs = 2 * e, 2 * e + 1
        up = e == 0
        arrived(xs, (0, 1, 3))
        arrived(xs, (0, 1, 1))
        onward(xs, 1, up)
        arrived(gs, (0, 0, 2))
        move(gs, (0, 0, 2), (0, 1, 2), y_pair)
        share(gs, 0)
        arrived(xs, (0, 0, 2))
        share(xs, 0)
    for e in range(2):
        xs, gs = 2 * e, 2 * e + 1
        arrived(xs, (0, 1, 2))
        share(xs, 1)
        for dz in range(4):
            arrived(gs, (0, 1, dz))
        share(gs, 1)

    c0, c1 = 0.7978845608028654, 0.044715
    pair = []
    for e in range(2):
        xs, gs = 2 * e, 2 * e + 1
        for s in (xs, gs):
            for dyl in range(2):
                arrive[s, "share", dyl].wait_recv()
        for n in range(3):
            loads[e * 3 + n].wait()
        step = hidden // 2
        for f in range(2):
            cols = pl.ds(f * step, step)
            pre_gate = dot(rows[xs], wg[e, :, cols], 1, 0)
            pre_up = dot(rows[xs], wu[e, :, cols], 1, 0)
            grad_hidden = dot(rows[gs], wd[e, cols, :], 1, 1)
            square = pre_gate * pre_gate
            t = jnp.tanh(c0 * (pre_gate + c1 * (pre_gate * square)))
            cdf = 0.5 * (1.0 + t)
            act = pre_gate * cdf
            slope = cdf + (0.5 * c0) * pre_gate * (1.0 - t * t) * (1.0 + (3.0 * c1) * square)
            hid_ref[e, :, cols] = (act * pre_up).astype(BF16)
            gu_ref[e, :, cols] = (grad_hidden * act).astype(BF16)
            gg_ref[e, :, cols] = (grad_hidden * pre_up * slope).astype(BF16)
        step = width // 4
        for d in range(4):
            cols = pl.ds(d * step, step)
            part = dot(gg_ref[e], wg[e, cols, :], 1, 1) + dot(gu_ref[e], wu[e, cols, :], 1, 1)
            acc[e, :, cols] = part[: 8 * TILE]
            pair_out[e, :, cols] = part[8 * TILE :].astype(BF16)
        pair.append(remote(pair_out.at[e], pair_in.at[e], sibling, fresh()))

    pair[0].wait_recv()
    acc[0] += pair_in[0].astype(F32)
    z2_out[0] = acc[0, 2 * TILE : 3 * TILE].astype(BF16)
    z2_out[1] = acc[0, 6 * TILE : 7 * TILE].astype(BF16)
    z2 = [
        remote(z2_out.at[0], z2_in.at[0], z_plus, fresh()),
        remote(z2_out.at[1], z2_in.at[1], z_minus, fresh()),
    ]
    zp_out[1] = acc[0, 5 * TILE : 6 * TILE].astype(BF16)
    zm_out[0] = acc[0, 3 * TILE : 4 * TILE].astype(BF16)
    zp = {1: remote(zp_out.at[1], zp_in.at[1], z_plus, fresh())}
    zm = {0: remote(zm_out.at[0], zm_in.at[0], z_minus, fresh())}

    pair[1].wait_recv()
    acc[1] += pair_in[1].astype(F32)
    y1_out[...] = acc[1, 4 * TILE : 8 * TILE].astype(BF16)
    y1 = remote(y1_out, y1_in, y_pair, fresh())

    z2[0].wait_recv()
    zp_out[0] = (acc[0, TILE : 2 * TILE] + z2_in[0].astype(F32)).astype(BF16)
    zp[0] = remote(zp_out.at[0], zp_in.at[0], z_plus, fresh())
    z2[1].wait_recv()
    zm_out[1] = (acc[0, 7 * TILE : 8 * TILE] + z2_in[1].astype(F32)).astype(BF16)
    zm[1] = remote(zm_out.at[1], zm_in.at[1], z_minus, fresh())

    y1.wait_recv()
    acc[1, 0 : 4 * TILE] += y1_in[...].astype(F32)
    z2_out[2] = acc[1, 2 * TILE : 3 * TILE].astype(BF16)
    z3 = [
        remote(z2_out.at[2, :, pl.ds(0, half)], z2_in.at[2, :, pl.ds(0, half)], z_plus, fresh()),
        remote(z2_out.at[2, :, pl.ds(half, half)], z2_in.at[2, :, pl.ds(half, half)], z_minus, fresh()),
    ]

    zp[1].wait_recv()
    zm[1].wait_recv()
    y0_out[...] = (
        acc[0, 4 * TILE : 5 * TILE] + zp_in[1].astype(F32) + zm_in[1].astype(F32)
    ).astype(BF16)
    y0 = remote(y0_out, y0_in, y_pair, fresh())

    z3[0].wait_recv()
    z3[1].wait_recv()
    zp_out[2, :, 0:half] = (
        acc[1, TILE : 2 * TILE, 0:half] + z2_in[2, :, 0:half].astype(F32)
    ).astype(BF16)
    zp_out[2, :, half:] = acc[1, TILE : 2 * TILE, half:].astype(BF16)
    zm_out[2, :, half:] = (
        acc[1, 3 * TILE : 4 * TILE, half:] + z2_in[2, :, half:].astype(F32)
    ).astype(BF16)
    zm_out[2, :, 0:half] = acc[1, 3 * TILE : 4 * TILE, 0:half].astype(BF16)
    zp[2] = remote(zp_out.at[2], zp_in.at[2], z_plus, fresh())
    zm[2] = remote(zm_out.at[2], zm_in.at[2], z_minus, fresh())

    zp[0].wait_recv()
    zm[0].wait_recv()
    y0.wait_recv()
    total0 = (
        acc[0, 0:TILE] + zp_in[0].astype(F32) + zm_in[0].astype(F32) + y0_in[...].astype(F32)
    )
    zp[2].wait_recv()
    zm[2].wait_recv()
    total1 = acc[1, 0:TILE] + zp_in[2].astype(F32) + zm_in[2].astype(F32)
    totals = jnp.concatenate([total0.astype(BF16), total1.astype(BF16)], axis=0)

    row_r = lax.broadcasted_iota(jnp.int32, (128, 32), 0)
    lane_r = lax.broadcasted_iota(jnp.int32, (128, 32), 1)
    from_row = ((row_r // 2) % 2) * 16 + (row_r // 16) * 2 + row_r % 2
    outgoing = None
    for q in range(4):
        choose = onehot((lane_r == from_row) & ((row_r // 4) % 4 == q))
        term = dot(choose, totals[:, q * quarter : (q + 1) * quarter], 1, 0)
        outgoing = term if outgoing is None else outgoing + term
    ret_out[...] = outgoing.astype(BF16)
    last = []
    for k in range(1, PEERS):
        part = pl.ds(k * TILE, TILE)
        last.append(remote(ret_out.at[part], ret_in.at[part], peer(k, -1), fresh()))
    ret_in[0:TILE] = ret_out[0:TILE]
    for copy in last:
        copy.wait_recv()
    both = match[0] + match[1]
    for q in range(4):
        choose = jnp.where((lane // 4) % 4 == q, both, 0.0).astype(BF16)
        gtok_ref[:, q * quarter : (q + 1) * quarter] = dot(choose, ret_in[...], 1, 0).astype(BF16)
    for copy in sent:
        copy.wait_send()


def weight_kernel(x_ref, g_ref, hid_ref, gg_ref, gu_ref, dgate_ref, dup_ref, ddown_ref):
    dgate_ref[0] = dot(x_ref[0], gg_ref[0], 0, 0).astype(BF16)
    dup_ref[0] = dot(x_ref[0], gu_ref[0], 0, 0).astype(BF16)
    ddown_ref[0] = dot(hid_ref[0], g_ref[0], 0, 0).astype(BF16)


def per_device(tokens, cotangent, route_weights, expert_ids, slot_ids, gate, up, down):
    local, width, hidden = gate.shape
    count = tokens.shape[0]
    total = BLOCKS * TILE
    vmem = pl.BlockSpec(memory_space=pltpu.VMEM)
    anywhere = pl.BlockSpec(memory_space=pl.ANY)
    grads, rows, hid, gg, gu = pl.pallas_call(
        main_kernel,
        out_shape=(
            jax.ShapeDtypeStruct((count, width), BF16),
            jax.ShapeDtypeStruct((4, total, width), BF16),
            jax.ShapeDtypeStruct((local, total, hidden), BF16),
            jax.ShapeDtypeStruct((local, total, hidden), BF16),
            jax.ShapeDtypeStruct((local, total, hidden), BF16),
        ),
        in_specs=[vmem] * 5 + [anywhere] * 3,
        out_specs=[vmem] * 5,
        scratch_shapes=[
            pltpu.VMEM((local, width, hidden), BF16),
            pltpu.VMEM((local, width, hidden), BF16),
            pltpu.VMEM((local, hidden, width), BF16),
            pltpu.VMEM((128, width // 2), BF16),
            pltpu.VMEM((128, width // 2), BF16),
            pltpu.VMEM((2, total // 2, width), F32),
            pltpu.VMEM((2, total // 2, width), BF16),
            pltpu.VMEM((2, total // 2, width), BF16),
            pltpu.VMEM((3, TILE, width), BF16),
            pltpu.VMEM((3, TILE, width), BF16),
            pltpu.VMEM((3, TILE, width), BF16),
            pltpu.VMEM((3, TILE, width), BF16),
            pltpu.VMEM((3, TILE, width), BF16),
            pltpu.VMEM((3, TILE, width), BF16),
            pltpu.VMEM((TILE, width), BF16),
            pltpu.VMEM((TILE, width), BF16),
            pltpu.VMEM((4 * TILE, width), BF16),
            pltpu.VMEM((4 * TILE, width), BF16),
            pltpu.VMEM((128, width // 4), BF16),
            pltpu.VMEM((128, width // 4), BF16),
            pltpu.SemaphoreType.DMA((6,)),
            pltpu.SemaphoreType.DMA((80,)),
            pltpu.SemaphoreType.DMA((80,)),
        ],
        compiler_params=pltpu.CompilerParams(
            collective_id=0, has_side_effects=True, vmem_limit_bytes=56 * 1024 * 1024
        ),
    )(tokens, cotangent, route_weights, expert_ids, slot_ids, gate, up, down)

    parts = 4
    step = width // parts
    row_block = (1, total, step)
    hid_spec = pl.BlockSpec((1, total, hidden), lambda e, d: (e, 0, 0))
    tall = pl.BlockSpec((1, step, hidden), lambda e, d: (e, d, 0))
    wide = pl.BlockSpec((1, hidden, step), lambda e, d: (e, 0, d))
    dgate, dup, ddown = pl.pallas_call(
        weight_kernel,
        grid=(local, parts),
        out_shape=(
            jax.ShapeDtypeStruct((local, width, hidden), BF16),
            jax.ShapeDtypeStruct((local, width, hidden), BF16),
            jax.ShapeDtypeStruct((local, hidden, width), BF16),
        ),
        in_specs=[
            pl.BlockSpec(row_block, lambda e, d: (2 * e, 0, d)),
            pl.BlockSpec(row_block, lambda e, d: (2 * e + 1, 0, d)),
            hid_spec,
            hid_spec,
            hid_spec,
        ],
        out_specs=[tall, tall, wide],
        compiler_params=pltpu.CompilerParams(vmem_limit_bytes=32 * 1024 * 1024),
    )(rows, rows, hid, gg, gu)
    return (grads, dgate, dup, ddown)


def solution(mesh):
    return jax.shard_map(
        per_device,
        mesh=mesh,
        in_specs=(
            P(("ex", "ey", "dp"), None),
            P(("ex", "ey", "dp"), None),
            P(("ex", "ey", "dp"), None),
            P(("ex", "ey", "dp"), None),
            P(("ex", "ey", "dp"), None),
            P("ex", None, ("ey", "dp")),
            P("ex", None, ("ey", "dp")),
            P("ex", ("ey", "dp"), None),
        ),
        out_specs=(
            P(("ex", "ey", "dp"), None),
            P("ex", None, ("ey", "dp")),
            P("ex", None, ("ey", "dp")),
            P("ex", ("ey", "dp"), None),
        ),
        check_vma=False,
    )
```

```python
import jax
import jax.numpy as jnp
from jax import lax
from jax.experimental import pallas as pl
from jax.experimental.pallas import tpu as pltpu
from jax.sharding import PartitionSpec as P

MESH = pl.DeviceIdType.MESH
F32 = jnp.float32
BF16 = jnp.bfloat16

NX = 4
NZ = 4
PEERS = 8
BLOCKS = 16
TILE = 16
HALF_ROWS = 8 * TILE


def dot(a, b, ca, cb):
    return lax.dot_general(a, b, (((ca,), (cb,)), ((), ())), preferred_element_type=F32)


def onehot(mask):
    return jnp.where(mask, 1.0, 0.0).astype(BF16)


def iota(shape, dim):
    return lax.broadcasted_iota(jnp.int32, shape, dim)


def block_row(dc, dyl, dz):
    return TILE * (dc * 8 + dyl * 4 + dz)


def main_kernel(
    tok_hbm, cot_hbm, rw_ref, ids_ref, slots_ref, wg_hbm, wu_hbm, wd_hbm,
    gtok_ref, dgate_ref, dup_ref, ddown_ref,
    tok_cot, rows, hid, gg, gu, pre, wg, wu, wd, send1, recv1, acc, pair_out, pair_in,
    back_out, back_in,
    ret_out, ret_in, load_sem, send_sem, recv_sem,
):
    ex, ey, dp = lax.axis_index("ex"), lax.axis_index("ey"), lax.axis_index("dp")
    yh, x = ex // NX, ex % NX
    yl, core = ey // 2, ey % 2
    width = rows.shape[2]
    half, quarter, eighth = width // 2, width // 4, width // 8
    hidden = wg.shape[2]

    def peer(k, sign):
        dyh, dx = k // NX, k % NX
        other_yl = (yl + dyh) % 2
        return (((yh + dyh) % 2) * NX + (x + sign * dx + NX) % NX, other_yl * 2 + core, dp)

    def mate(b):
        dyl, dz = b // NZ, b % NZ
        return (ex, (yl + dyl) % 2 * 2 + core, (dp + dz) % NZ)

    z_plus = (ex, ey, (dp + 1) % NZ)
    z_minus = (ex, ey, (dp + NZ - 1) % NZ)
    z_far = (ex, ey, (dp + 2) % NZ)
    y_pair = (ex, (1 - yl) * 2 + core, dp)
    sibling = (ex, yl * 2 + (1 - core), dp)

    barrier = pltpu.get_barrier_semaphore()
    partners = [peer(k, 1) for k in range(1, PEERS)] + [mate(b) for b in range(1, 8)] + [sibling]
    for device in partners:
        pl.semaphore_signal(barrier, inc=1, device_id=device, device_id_type=MESH)

    def load(src, dst, index):
        copy = pltpu.make_async_copy(src, dst, load_sem.at[index])
        copy.start()
        return copy

    tok_load = load(tok_hbm, tok_cot.at[0:16], 6)
    cot_load = load(cot_hbm, tok_cot.at[16:32], 7)
    weights = [
        load(src.at[e], dst.at[e], e * 3 + n)
        for e in range(2)
        for n, (src, dst) in enumerate(((wg_hbm, wg), (wu_hbm, wu), (wd_hbm, wd)))
    ]

    count = [0, 0]
    sent = []

    def remote(src, dst, device):
        copy = pltpu.make_async_remote_copy(
            src_ref=src,
            dst_ref=dst,
            send_sem=send_sem.at[count[0]],
            recv_sem=recv_sem.at[count[0]],
            device_id=device,
            device_id_type=MESH,
        )
        count[0] += 1
        copy.start()
        sent.append(copy)
        return copy

    ids, slots, rw = ids_ref[...], slots_ref[...], rw_ref[...]
    row = iota((128, 16), 0)
    piece = row // 16
    group = ((yh + piece // NX) % 2) * NX + (x + piece % NX) % NX

    def matches(e):
        expert, slot = group * 2 + e, row % 2
        return [
            jnp.where((ids[k : k + 1] == expert) & (slots[k : k + 1] == slot), 1.0, 0.0)
            for k in range(2)
        ]

    def build(e):
        m = matches(e)
        is_grad = (row // 2) % 2 == 1
        any_match = m[0] + m[1]
        scale = jnp.sum(m[0] * rw[0:1] + m[1] * rw[1:2], axis=1, keepdims=True)
        scale = jnp.where(is_grad[:, 0:1], scale, 1.0)
        pick = jnp.concatenate(
            [jnp.where(is_grad, 0.0, any_match), jnp.where(is_grad, any_match, 0.0)], axis=1
        )
        part_of = (iota((128, 32), 0) // 4) % 4
        total = None
        for q in range(4):
            choose = jnp.where(part_of == q, pick, 0.0).astype(BF16)
            term = dot(choose, tok_cot[:, q * quarter : (q + 1) * quarter], 1, 0)
            total = term if total is None else total + term
        send1[e] = (total * scale).astype(BF16)

    first = {}

    def over_ex(e):
        first[e] = []
        for k in range(1, PEERS):
            part = pl.ds(k * TILE, TILE)
            first[e].append(remote(send1.at[e, part], recv1.at[e, part], peer(k, 1)))
        recv1[e, 0:TILE] = send1[e, 0:TILE]

    def form(e):
        for copy in first[e]:
            copy.wait_recv()
        out, lane = iota((32, 128), 0), iota((32, 128), 1)
        source = ((out % 16) // 2) * 16 + (out // 16) * 2 + out % 2
        for q in range(4):
            block = dot(onehot(lane == source + 4 * q), recv1[e], 1, 0).astype(BF16)
            cols = slice(q * quarter, (q + 1) * quarter)
            rows[2 * e, 0:TILE, cols] = block[0:TILE]
            rows[2 * e + 1, 0:TILE, cols] = block[TILE:]

    arrive = {}

    def move(s, here, there, device):
        src = rows.at[s, pl.ds(block_row(*here), TILE)]
        dst = rows.at[s, pl.ds(block_row(*there), TILE)]
        arrive[s, there] = remote(src, dst, device)

    def share(s, dyl, dz):
        move(s, (0, dyl, dz), (1, dyl, dz), sibling)

    def arrived(s, *block):
        arrive[s, block].wait_recv()

    def around(s, dyl):
        move(s, (0, dyl, 0), (0, dyl, 3), z_plus)
        move(s, (0, dyl, 0), (0, dyl, 1), z_minus)
        move(s, (0, dyl, 0), (0, dyl, 2), z_far)

    def across(s, dz):
        move(s, (0, 0, dz), (0, 1, dz), y_pair)

    def pass_on(s, dyl, dz):
        arrived(s, 0, dyl, dz)
        share(s, dyl, dz)

    def pass_across(s, dz):
        arrived(s, 0, 0, dz)
        across(s, dz)
        share(s, 0, dz)

    def shared(s):
        for dyl in range(2):
            for dz in range(4):
                arrived(s, 1, dyl, dz)

    c0, c1 = 0.7978845608028654, 0.044715
    step = hidden // 2

    def forward_inputs(e, f):
        cols = pl.ds(f * step, step)
        pre[0, :, cols] = dot(rows[2 * e], wg[e, :, cols], 1, 0)
        pre[1, :, cols] = dot(rows[2 * e], wu[e, :, cols], 1, 0)

    def forward_grads(e, f):
        cols = pl.ds(f * step, step)
        grad_hidden = dot(rows[2 * e + 1], wd[e, cols, :], 1, 1)
        pre_gate, pre_up = pre[0, :, cols], pre[1, :, cols]
        square = pre_gate * pre_gate
        t = jnp.tanh(c0 * (pre_gate + c1 * (pre_gate * square)))
        cdf = 0.5 * (1.0 + t)
        act = pre_gate * cdf
        slope = cdf + (0.5 * c0) * pre_gate * (1.0 - t * t) * (1.0 + (3.0 * c1) * square)
        hid[e, :, cols] = (act * pre_up).astype(BF16)
        gu[e, :, cols] = (grad_hidden * act).astype(BF16)
        gg[e, :, cols] = (grad_hidden * pre_up * slope).astype(BF16)

    pair = {}

    def input_grad(e, d):
        cols = pl.ds(d * quarter, quarter)
        part = dot(gg[e], wg[e, cols, :], 1, 1) + dot(gu[e], wu[e, cols, :], 1, 1)
        pair_out[e, :, cols] = part[HALF_ROWS:].astype(BF16)
        acc[e, :, cols] = part[:HALF_ROWS]
        pair[e, d] = remote(pair_out.at[e, :, cols], pair_in.at[e, :, cols], sibling)

    def weight_grad(e, which):
        if which == 0:
            dgate_ref[e] = dot(rows[2 * e], gg[e], 0, 0).astype(BF16)
        elif which == 1:
            dup_ref[e] = dot(rows[2 * e], gu[e], 0, 0).astype(BF16)
        else:
            ddown_ref[e] = dot(hid[e], rows[2 * e + 1], 0, 0).astype(BF16)

    hop = {}

    def send_back(e, h):
        for d in (2 * h, 2 * h + 1):
            pair[e, d].wait_recv()
        cols = pl.ds(h * half, half)
        both = acc[e, :, cols] + pair_in[e, :, cols].astype(F32)
        acc[e, 0:TILE, cols] = both[0:TILE]
        back_out[e, TILE:, cols] = both[TILE:].astype(BF16)
        for b in (6, 5, 7, 2, 4, 1, 3):
            block = pl.ds(b * TILE, TILE)
            hop[e, h, b] = remote(
                back_out.at[e, block, cols], back_in.at[e, block, cols], mate(b)
            )

    def back_over_ex(e):
        for h in range(2):
            for b in range(1, 8):
                hop[e, h, b].wait_recv()
        summed = acc[e, 0:TILE]
        for b in range(1, 8):
            summed += back_in[e, b * TILE : (b + 1) * TILE].astype(F32)
        summed = summed.astype(BF16)
        out, lane = iota((128, TILE), 0), iota((128, TILE), 1)
        fits = lane == (out // 16) * 2 + out % 2
        total = None
        for q in range(8):
            choose = onehot(fits & ((out // 2) % 8 == q))
            term = dot(choose, summed[:, q * eighth : (q + 1) * eighth], 1, 0)
            total = term if total is None else total + term
        ret_out[e] = total.astype(BF16)
        for k in range(1, PEERS):
            part = pl.ds(k * TILE, TILE)
            into = ret_in.at[pl.ds(e * 128 + k * TILE, TILE)]
            hop[e, k] = remote(ret_out.at[e, part], into, peer(k, -1))
        ret_in[e * 128 : e * 128 + TILE] = ret_out[e, 0:TILE]

    def combine():
        pick = []
        for e in range(2):
            m = matches(e)
            pick.append(m[0] + m[1])
        pick = jnp.concatenate(pick, axis=0)
        part_of = (iota((256, 16), 0) // 2) % 8
        chosen = [jnp.where(part_of == q, pick, 0.0).astype(BF16) for q in range(8)]
        for e in range(2):
            for k in range(1, PEERS):
                hop[e, k].wait_recv()
        for q in range(8):
            gtok_ref[:, q * eighth : (q + 1) * eighth] = dot(
                chosen[q], ret_in[...], 0, 0
            ).astype(BF16)

    tok_load.wait()
    cot_load.wait()
    build(0)
    pl.semaphore_wait(barrier, len(partners))
    over_ex(0)
    build(1)
    over_ex(1)
    form(0)
    across(0, 0)
    around(1, 0)
    around(0, 0)
    across(1, 0)
    share(0, 0, 0)
    share(1, 0, 0)
    form(1)
    across(2, 0)
    around(3, 0)
    across(3, 0)
    share(2, 0, 0)
    share(3, 0, 0)
    arrived(0, 0, 1, 0)
    around(0, 1)
    share(0, 1, 0)
    around(2, 0)
    for dz in (3, 1, 2):
        pass_across(1, dz)
    for dz in (3, 1, 2):
        pass_on(0, 0, dz)
    pass_on(1, 1, 0)
    arrived(2, 0, 1, 0)
    around(2, 1)
    share(2, 1, 0)
    for dz in (3, 1, 2):
        pass_across(3, dz)
    for dz in (3, 1, 2):
        pass_on(0, 1, dz)
    for dz in (3, 1, 2):
        pass_on(1, 1, dz)
    shared(0)
    for n in range(3):
        weights[n].wait()
    forward_inputs(0, 0)
    forward_inputs(0, 1)
    for dz in (3, 1, 2):
        pass_on(2, 0, dz)
    pass_on(3, 1, 0)
    shared(1)
    forward_grads(0, 0)
    forward_grads(0, 1)
    for d in range(2):
        input_grad(0, d)
    for dz in (3, 1, 2):
        pass_on(2, 1, dz)
    for d in range(2, 4):
        input_grad(0, d)
    for dz in (3, 1, 2):
        pass_on(3, 1, dz)
    send_back(0, 0)
    send_back(0, 1)
    for n in range(3, 6):
        weights[n].wait()
    shared(2)
    forward_inputs(1, 0)
    forward_inputs(1, 1)
    shared(3)
    forward_grads(1, 0)
    forward_grads(1, 1)
    input_grad(1, 0)
    input_grad(1, 1)
    input_grad(1, 2)
    input_grad(1, 3)
    weight_grad(0, 0)
    send_back(1, 0)
    send_back(1, 1)
    weight_grad(0, 1)
    back_over_ex(0)
    weight_grad(0, 2)
    weight_grad(1, 0)
    weight_grad(1, 1)
    back_over_ex(1)
    weight_grad(1, 2)
    combine()
    for copy in sent:
        copy.wait_send()


def write_kernel(a_ref, b_ref, c_ref, d_ref, a_hbm, b_hbm, c_hbm, d_hbm, sem):
    copies = [
        pltpu.make_async_copy(src, dst, sem.at[n])
        for n, (src, dst) in enumerate(
            ((a_ref, a_hbm), (b_ref, b_hbm), (c_ref, c_hbm), (d_ref, d_hbm))
        )
    ]
    for copy in copies:
        copy.start()
    for copy in copies:
        copy.wait()


def per_device(tokens, cotangent, route_weights, expert_ids, slot_ids, gate, up, down):
    local, width, hidden = gate.shape
    count = tokens.shape[0]
    total = BLOCKS * TILE
    vmem = pl.BlockSpec(memory_space=pltpu.VMEM)
    hbm = pl.BlockSpec(memory_space=pltpu.HBM)
    results = pl.pallas_call(
        main_kernel,
        out_shape=(
            pltpu.VMEM((count, width), BF16),
            pltpu.VMEM((local, width, hidden), BF16),
            pltpu.VMEM((local, width, hidden), BF16),
            pltpu.VMEM((local, hidden, width), BF16),
        ),
        in_specs=[hbm] * 2 + [vmem] * 3 + [hbm] * 3,
        out_specs=[vmem] * 4,
        scratch_shapes=[
            pltpu.VMEM((2 * count, width), BF16),
            pltpu.VMEM((4, total, width), BF16),
            pltpu.VMEM((local, total, hidden), BF16),
            pltpu.VMEM((local, total, hidden), BF16),
            pltpu.VMEM((local, total, hidden), BF16),
            pltpu.VMEM((2, total, hidden), F32),
            pltpu.VMEM((local, width, hidden), BF16),
            pltpu.VMEM((local, width, hidden), BF16),
            pltpu.VMEM((local, hidden, width), BF16),
            pltpu.VMEM((2, 128, width // 4), BF16),
            pltpu.VMEM((2, 128, width // 4), BF16),
            pltpu.VMEM((2, HALF_ROWS, width), F32),
            pltpu.VMEM((2, HALF_ROWS, width), BF16),
            pltpu.VMEM((2, HALF_ROWS, width), BF16),
            pltpu.VMEM((2, HALF_ROWS, width), BF16),
            pltpu.VMEM((2, HALF_ROWS, width), BF16),
            pltpu.VMEM((2, 128, width // 8), BF16),
            pltpu.VMEM((256, width // 8), BF16),
            pltpu.SemaphoreType.DMA((8,)),
            pltpu.SemaphoreType.DMA((150,)),
            pltpu.SemaphoreType.DMA((150,)),
        ],
        compiler_params=pltpu.CompilerParams(
            collective_id=0, has_side_effects=True, vmem_limit_bytes=46 * 1024 * 1024
        ),
    )(tokens, cotangent, route_weights.T, expert_ids.T, slot_ids.T, gate, up, down)
    return pl.pallas_call(
        write_kernel,
        out_shape=tuple(jax.ShapeDtypeStruct(a.shape, BF16) for a in results),
        in_specs=[vmem] * 4,
        out_specs=[hbm] * 4,
        scratch_shapes=[pltpu.SemaphoreType.DMA((4,))],
        compiler_params=pltpu.CompilerParams(vmem_limit_bytes=4 * 1024 * 1024),
    )(*results)


def solution(mesh):
    return jax.shard_map(
        per_device,
        mesh=mesh,
        in_specs=(
            P(("ex", "ey", "dp"), None),
            P(("ex", "ey", "dp"), None),
            P(("ex", "ey", "dp"), None),
            P(("ex", "ey", "dp"), None),
            P(("ex", "ey", "dp"), None),
            P("ex", None, ("ey", "dp")),
            P("ex", None, ("ey", "dp")),
            P("ex", ("ey", "dp"), None),
        ),
        out_specs=(
            P(("ex", "ey", "dp"), None),
            P("ex", None, ("ey", "dp")),
            P("ex", None, ("ey", "dp")),
            P("ex", ("ey", "dp"), None),
        ),
        check_vma=False,
    )
```

```python
import jax
import jax.numpy as jnp
from jax import lax
from jax.experimental import pallas as pl
from jax.experimental.pallas import tpu as pltpu
from jax.sharding import PartitionSpec as P

MESH = pl.DeviceIdType.MESH
F32 = jnp.float32
BF16 = jnp.bfloat16

NX = 4
NZ = 4
PEERS = 8
BLOCKS = 16
TILE = 16
HALF_ROWS = 8 * TILE


def dot(a, b, ca, cb):
    return lax.dot_general(a, b, (((ca,), (cb,)), ((), ())), preferred_element_type=F32)


def onehot(mask):
    return jnp.where(mask, 1.0, 0.0).astype(BF16)


def iota(shape, dim):
    return lax.broadcasted_iota(jnp.int32, shape, dim)


def block_row(dc, dyl, dz):
    return TILE * (dc * 8 + dyl * 4 + dz)


def main_kernel(
    tok_hbm, cot_hbm, rw_ref, ids_ref, slots_ref, wg_hbm, wu_hbm, wd_hbm,
    gtok_ref, dgate_ref, dup_ref, ddown_ref,
    tok_cot, rows, hid, gg, gu, pre, wg, wu, wd, send1, recv1, acc, pair_out, pair_in,
    back_out, back_in,
    ret_out, ret_in, load_sem, send_sem, recv_sem,
):
    ex, ey, dp = lax.axis_index("ex"), lax.axis_index("ey"), lax.axis_index("dp")
    yh, x = ex // NX, ex % NX
    yl, core = ey // 2, ey % 2
    width = rows.shape[2]
    half, quarter, eighth = width // 2, width // 4, width // 8
    hidden = wg.shape[2]

    def peer(k, sign):
        dyh, dx = k // NX, k % NX
        other_yl = (yl + dyh) % 2
        return (((yh + dyh) % 2) * NX + (x + sign * dx + NX) % NX, other_yl * 2 + core, dp)

    def mate(b):
        dyl, dz = b // NZ, b % NZ
        return (ex, (yl + dyl) % 2 * 2 + core, (dp + dz) % NZ)

    z_plus = (ex, ey, (dp + 1) % NZ)
    z_minus = (ex, ey, (dp + NZ - 1) % NZ)
    z_far = (ex, ey, (dp + 2) % NZ)
    y_pair = (ex, (1 - yl) * 2 + core, dp)
    sibling = (ex, yl * 2 + (1 - core), dp)

    barrier = pltpu.get_barrier_semaphore()
    partners = [peer(k, 1) for k in range(1, PEERS)] + [mate(b) for b in range(1, 8)] + [sibling]
    for device in partners:
        pl.semaphore_signal(barrier, inc=1, device_id=device, device_id_type=MESH)

    def load(src, dst, index):
        copy = pltpu.make_async_copy(src, dst, load_sem.at[index])
        copy.start()
        return copy

    tok_load = load(tok_hbm, tok_cot.at[0:16], 6)
    cot_load = load(cot_hbm, tok_cot.at[16:32], 7)
    weights = [
        load(src.at[e], dst.at[e], e * 3 + n)
        for e in range(2)
        for n, (src, dst) in enumerate(((wg_hbm, wg), (wu_hbm, wu), (wd_hbm, wd)))
    ]

    count = [0, 0]
    sent = []

    def remote(src, dst, device):
        copy = pltpu.make_async_remote_copy(
            src_ref=src,
            dst_ref=dst,
            send_sem=send_sem.at[count[0]],
            recv_sem=recv_sem.at[count[0]],
            device_id=device,
            device_id_type=MESH,
        )
        count[0] += 1
        copy.start()
        sent.append(copy)
        return copy

    ids, slots, rw = [
        jnp.concatenate([ref[...]] * 8, axis=1) for ref in (ids_ref, slots_ref, rw_ref)
    ]
    row, lane = iota((128, 128), 0), iota((128, 128), 1)
    piece = row // 16
    group = ((yh + piece // NX) % 2) * NX + (x + piece % NX) % NX

    def matches(e, k, also):
        fits = (ids[k : k + 1] == group * 2 + e) & (slots[k : k + 1] == row % 2) & also
        return jnp.where(fits, 1.0, 0.0)

    def stacked(array, parts):
        size = array.shape[1] // parts
        return jnp.concatenate([array[:, n * size : (n + 1) * size] for n in range(parts)], axis=0)

    def build(e):
        is_grad = (row // 2) % 2
        also = (lane // 32 == (row // 4) % 4) & ((lane // 16) % 2 == is_grad)
        m = [matches(e, k, also) for k in range(2)]
        scale = jnp.sum(m[0] * rw[0:1] + m[1] * rw[1:2], axis=1, keepdims=True)
        scale = jnp.where(is_grad[:, 0:1] == 1, scale, 1.0)
        picked = dot((m[0] + m[1]).astype(BF16), stacked(tok_cot[...], 4), 1, 0)
        send1[e] = (picked * scale).astype(BF16)

    first = {}

    def over_ex(e):
        first[e] = []
        for k in (6, 2, 5, 7, 4, 1, 3):
            part = pl.ds(k * TILE, TILE)
            first[e].append(remote(send1.at[e, part], recv1.at[e, part], peer(k, 1)))
        recv1[e, 0:TILE] = send1[e, 0:TILE]

    regroup = onehot(
        lane == ((row % 16) // 2) * 16 + (row // 32) * 4 + ((row // 16) % 2) * 2 + row % 2
    )

    def form(e):
        for copy in first[e]:
            copy.wait_recv()
        block = dot(regroup, recv1[e], 1, 0).astype(BF16)
        for q in range(4):
            cols = slice(q * quarter, (q + 1) * quarter)
            rows[2 * e, 0:TILE, cols] = block[q * 32 : q * 32 + 16]
            rows[2 * e + 1, 0:TILE, cols] = block[q * 32 + 16 : q * 32 + 32]

    arrive = {}

    def move(s, here, there, device):
        src = rows.at[s, pl.ds(block_row(*here), TILE)]
        dst = rows.at[s, pl.ds(block_row(*there), TILE)]
        arrive[s, there] = remote(src, dst, device)

    def share(s, dyl, dz):
        move(s, (0, dyl, dz), (1, dyl, dz), sibling)

    def arrived(s, *block):
        arrive[s, block].wait_recv()

    def around(s, dyl):
        move(s, (0, dyl, 0), (0, dyl, 3), z_plus)
        move(s, (0, dyl, 0), (0, dyl, 1), z_minus)
        move(s, (0, dyl, 0), (0, dyl, 2), z_far)

    def across(s, dz):
        move(s, (0, 0, dz), (0, 1, dz), y_pair)

    def pass_on(s, dyl, dz):
        arrived(s, 0, dyl, dz)
        share(s, dyl, dz)

    def pass_across(s, dz):
        arrived(s, 0, 0, dz)
        across(s, dz)
        share(s, 0, dz)

    def shared(s):
        for dyl in range(2):
            for dz in range(4):
                arrived(s, 1, dyl, dz)

    c0, c1 = 0.7978845608028654, 0.044715
    step = hidden // 2

    def forward_inputs(e, f):
        cols = pl.ds(f * step, step)
        pre[0, :, cols] = dot(rows[2 * e], wg[e, :, cols], 1, 0)
        pre[1, :, cols] = dot(rows[2 * e], wu[e, :, cols], 1, 0)

    def forward_grads(e, f):
        cols = pl.ds(f * step, step)
        grad_hidden = dot(rows[2 * e + 1], wd[e, cols, :], 1, 1)
        pre_gate, pre_up = pre[0, :, cols], pre[1, :, cols]
        square = pre_gate * pre_gate
        t = jnp.tanh(c0 * (pre_gate + c1 * (pre_gate * square)))
        cdf = 0.5 * (1.0 + t)
        act = pre_gate * cdf
        slope = cdf + (0.5 * c0) * pre_gate * (1.0 - t * t) * (1.0 + (3.0 * c1) * square)
        hid[e, :, cols] = (act * pre_up).astype(BF16)
        gu[e, :, cols] = (grad_hidden * act).astype(BF16)
        gg[e, :, cols] = (grad_hidden * pre_up * slope).astype(BF16)

    pair = {}

    def input_grad(e, d):
        cols = pl.ds(d * quarter, quarter)
        part = dot(gg[e], wg[e, cols, :], 1, 1) + dot(gu[e], wu[e, cols, :], 1, 1)
        pair_out[e, :, cols] = part[HALF_ROWS:].astype(BF16)
        acc[e, :, cols] = part[:HALF_ROWS]
        pair[e, d] = remote(pair_out.at[e, :, cols], pair_in.at[e, :, cols], sibling)

    def weight_grad(e, which):
        if which == 0:
            dgate_ref[e] = dot(rows[2 * e], gg[e], 0, 0).astype(BF16)
        elif which == 1:
            dup_ref[e] = dot(rows[2 * e], gu[e], 0, 0).astype(BF16)
        else:
            ddown_ref[e] = dot(hid[e], rows[2 * e + 1], 0, 0).astype(BF16)

    hop = {}

    def send_back(e, h):
        for d in (2 * h, 2 * h + 1):
            pair[e, d].wait_recv()
        cols = pl.ds(h * half, half)
        both = acc[e, :, cols] + pair_in[e, :, cols].astype(F32)
        acc[e, 0:TILE, cols] = both[0:TILE]
        back_out[e, TILE:, cols] = both[TILE:].astype(BF16)
        for b in (6, 5, 7, 2, 4, 1, 3):
            block = pl.ds(b * TILE, TILE)
            hop[e, h, b] = remote(
                back_out.at[e, block, cols], back_in.at[e, block, cols], mate(b)
            )

    ungroup = onehot(lane == ((row // 2) % 8) * 16 + (row // 16) * 2 + row % 2)

    def back_over_ex(e):
        for h in range(2):
            for b in range(1, 8):
                hop[e, h, b].wait_recv()
        summed = acc[e, 0:TILE]
        for b in range(1, 8):
            summed += back_in[e, b * TILE : (b + 1) * TILE].astype(F32)
        summed = summed.astype(BF16)
        ret_out[e] = dot(ungroup, stacked(summed, 8), 1, 0).astype(BF16)
        for k in (6, 2, 5, 7, 4, 1, 3):
            part = pl.ds(k * TILE, TILE)
            into = ret_in.at[pl.ds(e * 128 + k * TILE, TILE)]
            hop[e, k] = remote(ret_out.at[e, part], into, peer(k, -1))
        ret_in[e * 128 : e * 128 + TILE] = ret_out[e, 0:TILE]

    def combine():
        here = lane // 16 == (row // 2) % 8
        pick = jnp.concatenate(
            [(matches(e, 0, here) + matches(e, 1, here)).astype(BF16) for e in range(2)], axis=0
        )
        for e in range(2):
            for k in range(1, PEERS):
                hop[e, k].wait_recv()
        out = dot(pick, ret_in[...], 0, 0).astype(BF16)
        for q in range(8):
            gtok_ref[:, q * eighth : (q + 1) * eighth] = out[q * 16 : (q + 1) * 16]

    tok_load.wait()
    cot_load.wait()
    build(0)
    pl.semaphore_wait(barrier, len(partners))
    over_ex(0)
    build(1)
    over_ex(1)
    form(0)
    across(0, 0)
    around(1, 0)
    around(0, 0)
    across(1, 0)
    share(0, 0, 0)
    share(1, 0, 0)
    form(1)
    across(2, 0)
    around(3, 0)
    across(3, 0)
    share(2, 0, 0)
    share(3, 0, 0)
    arrived(0, 0, 1, 0)
    around(0, 1)
    share(0, 1, 0)
    around(2, 0)
    for dz in (3, 1, 2):
        pass_across(1, dz)
    for dz in (3, 1, 2):
        pass_on(0, 0, dz)
    pass_on(1, 1, 0)
    arrived(2, 0, 1, 0)
    around(2, 1)
    share(2, 1, 0)
    for dz in (3, 1, 2):
        pass_across(3, dz)
    for dz in (3, 1, 2):
        pass_on(0, 1, dz)
    for dz in (3, 1, 2):
        pass_on(1, 1, dz)
    shared(0)
    for n in range(3):
        weights[n].wait()
    forward_inputs(0, 0)
    forward_inputs(0, 1)
    for dz in (3, 1, 2):
        pass_on(2, 0, dz)
    pass_on(3, 1, 0)
    shared(1)
    forward_grads(0, 0)
    forward_grads(0, 1)
    for d in range(2):
        input_grad(0, d)
    for dz in (3, 1, 2):
        pass_on(2, 1, dz)
    for d in range(2, 4):
        input_grad(0, d)
    for dz in (3, 1, 2):
        pass_on(3, 1, dz)
    send_back(0, 0)
    send_back(0, 1)
    for n in range(3, 6):
        weights[n].wait()
    shared(2)
    forward_inputs(1, 0)
    forward_inputs(1, 1)
    shared(3)
    forward_grads(1, 0)
    forward_grads(1, 1)
    input_grad(1, 0)
    input_grad(1, 1)
    input_grad(1, 2)
    input_grad(1, 3)
    send_back(1, 0)
    send_back(1, 1)
    weight_grad(0, 0)
    back_over_ex(0)
    weight_grad(0, 1)
    weight_grad(0, 2)
    weight_grad(1, 0)
    weight_grad(1, 1)
    back_over_ex(1)
    weight_grad(1, 2)
    combine()
    for copy in sent:
        copy.wait_send()


def write_kernel(a_ref, b_ref, c_ref, d_ref, a_hbm, b_hbm, c_hbm, d_hbm, sem):
    copies = [
        pltpu.make_async_copy(src, dst, sem.at[n])
        for n, (src, dst) in enumerate(
            ((a_ref, a_hbm), (b_ref, b_hbm), (c_ref, c_hbm), (d_ref, d_hbm))
        )
    ]
    for copy in copies:
        copy.start()
    for copy in copies:
        copy.wait()


def per_device(tokens, cotangent, route_weights, expert_ids, slot_ids, gate, up, down):
    local, width, hidden = gate.shape
    count = tokens.shape[0]
    total = BLOCKS * TILE
    vmem = pl.BlockSpec(memory_space=pltpu.VMEM)
    hbm = pl.BlockSpec(memory_space=pltpu.HBM)
    results = pl.pallas_call(
        main_kernel,
        out_shape=(
            pltpu.VMEM((count, width), BF16),
            pltpu.VMEM((local, width, hidden), BF16),
            pltpu.VMEM((local, width, hidden), BF16),
            pltpu.VMEM((local, hidden, width), BF16),
        ),
        in_specs=[hbm] * 2 + [vmem] * 3 + [hbm] * 3,
        out_specs=[vmem] * 4,
        scratch_shapes=[
            pltpu.VMEM((2 * count, width), BF16),
            pltpu.VMEM((4, total, width), BF16),
            pltpu.VMEM((local, total, hidden), BF16),
            pltpu.VMEM((local, total, hidden), BF16),
            pltpu.VMEM((local, total, hidden), BF16),
            pltpu.VMEM((2, total, hidden), F32),
            pltpu.VMEM((local, width, hidden), BF16),
            pltpu.VMEM((local, width, hidden), BF16),
            pltpu.VMEM((local, hidden, width), BF16),
            pltpu.VMEM((2, 128, width // 4), BF16),
            pltpu.VMEM((2, 128, width // 4), BF16),
            pltpu.VMEM((2, HALF_ROWS, width), F32),
            pltpu.VMEM((2, HALF_ROWS, width), BF16),
            pltpu.VMEM((2, HALF_ROWS, width), BF16),
            pltpu.VMEM((2, HALF_ROWS, width), BF16),
            pltpu.VMEM((2, HALF_ROWS, width), BF16),
            pltpu.VMEM((2, 128, width // 8), BF16),
            pltpu.VMEM((256, width // 8), BF16),
            pltpu.SemaphoreType.DMA((8,)),
            pltpu.SemaphoreType.DMA((150,)),
            pltpu.SemaphoreType.DMA((150,)),
        ],
        compiler_params=pltpu.CompilerParams(
            collective_id=0, has_side_effects=True, vmem_limit_bytes=46 * 1024 * 1024
        ),
    )(tokens, cotangent, route_weights.T, expert_ids.T, slot_ids.T, gate, up, down)
    return pl.pallas_call(
        write_kernel,
        out_shape=tuple(jax.ShapeDtypeStruct(a.shape, BF16) for a in results),
        in_specs=[vmem] * 4,
        out_specs=[hbm] * 4,
        scratch_shapes=[pltpu.SemaphoreType.DMA((4,))],
        compiler_params=pltpu.CompilerParams(vmem_limit_bytes=4 * 1024 * 1024),
    )(*results)


def solution(mesh):
    return jax.shard_map(
        per_device,
        mesh=mesh,
        in_specs=(
            P(("ex", "ey", "dp"), None),
            P(("ex", "ey", "dp"), None),
            P(("ex", "ey", "dp"), None),
            P(("ex", "ey", "dp"), None),
            P(("ex", "ey", "dp"), None),
            P("ex", None, ("ey", "dp")),
            P("ex", None, ("ey", "dp")),
            P("ex", ("ey", "dp"), None),
        ),
        out_specs=(
            P(("ex", "ey", "dp"), None),
            P("ex", None, ("ey", "dp")),
            P("ex", None, ("ey", "dp")),
            P("ex", ("ey", "dp"), None),
        ),
        check_vma=False,
    )
```

```python
import jax
import jax.numpy as jnp
from jax import lax
from jax.experimental import pallas as pl
from jax.experimental.pallas import tpu as pltpu
from jax.sharding import PartitionSpec as P

MESH = pl.DeviceIdType.MESH
F32 = jnp.float32
BF16 = jnp.bfloat16

NX = 4
NZ = 4
PEERS = 8
BLOCKS = 16
TILE = 16
HALF_ROWS = 8 * TILE


def dot(a, b, ca, cb):
    return lax.dot_general(a, b, (((ca,), (cb,)), ((), ())), preferred_element_type=F32)


def onehot(mask):
    return jnp.where(mask, 1.0, 0.0).astype(BF16)


def iota(shape, dim):
    return lax.broadcasted_iota(jnp.int32, shape, dim)


def block_row(dc, dyl, dz):
    return TILE * (dc * 8 + dyl * 4 + dz)


def main_kernel(
    tok_hbm, cot_hbm, rw_ref, ids_ref, slots_ref, wg_hbm, wu_hbm, wd_hbm,
    gtok_ref, dgate_ref, dup_ref, ddown_ref,
    tok_cot, rows, hid, gg, gu, pre, wg, wu, wd, send1, recv1, acc, pair_out, pair_in,
    back_out, back_in,
    ret_out, ret_in, load_sem, send_sem, recv_sem,
):
    ex, ey, dp = lax.axis_index("ex"), lax.axis_index("ey"), lax.axis_index("dp")
    yh, x = ex // NX, ex % NX
    yl, core = ey // 2, ey % 2
    width = rows.shape[2]
    half, quarter, eighth = width // 2, width // 4, width // 8
    hidden = wg.shape[2]

    def peer(k, sign):
        dyh, dx = k // NX, k % NX
        other_yl = (yl + dyh) % 2
        return (((yh + dyh) % 2) * NX + (x + sign * dx + NX) % NX, other_yl * 2 + core, dp)

    def mate(b):
        dyl, dz = b // NZ, b % NZ
        return (ex, (yl + dyl) % 2 * 2 + core, (dp + dz) % NZ)

    z_plus = (ex, ey, (dp + 1) % NZ)
    z_minus = (ex, ey, (dp + NZ - 1) % NZ)
    z_far = (ex, ey, (dp + 2) % NZ)
    y_pair = (ex, (1 - yl) * 2 + core, dp)
    sibling = (ex, yl * 2 + (1 - core), dp)

    barrier = pltpu.get_barrier_semaphore()
    partners = [peer(k, 1) for k in range(1, PEERS)] + [mate(b) for b in range(1, 8)] + [sibling]
    for device in partners:
        pl.semaphore_signal(barrier, inc=1, device_id=device, device_id_type=MESH)

    def load(src, dst, index):
        copy = pltpu.make_async_copy(src, dst, load_sem.at[index])
        copy.start()
        return copy

    tok_load = load(tok_hbm, tok_cot.at[0:16], 6)
    cot_load = load(cot_hbm, tok_cot.at[16:32], 7)
    weights = [
        load(src.at[e], dst.at[e], e * 3 + n)
        for e in range(2)
        for n, (src, dst) in enumerate(((wg_hbm, wg), (wu_hbm, wu), (wd_hbm, wd)))
    ]

    count = [0, 0]
    sent = []

    def remote(src, dst, device):
        copy = pltpu.make_async_remote_copy(
            src_ref=src,
            dst_ref=dst,
            send_sem=send_sem.at[count[0]],
            recv_sem=recv_sem.at[count[0]],
            device_id=device,
            device_id_type=MESH,
        )
        count[0] += 1
        copy.start()
        sent.append(copy)
        return copy

    ids, slots, rw = [
        jnp.concatenate([ref[...]] * 8, axis=1) for ref in (ids_ref, slots_ref, rw_ref)
    ]
    row, lane = iota((128, 128), 0), iota((128, 128), 1)
    piece = row // 16
    group = ((yh + piece // NX) % 2) * NX + (x + piece % NX) % NX

    def matches(e, k, also):
        fits = (ids[k : k + 1] == group * 2 + e) & (slots[k : k + 1] == row % 2) & also
        return jnp.where(fits, 1.0, 0.0)

    def stacked(array, parts):
        size = array.shape[1] // parts
        return jnp.concatenate([array[:, n * size : (n + 1) * size] for n in range(parts)], axis=0)

    def build(e):
        is_grad = (row // 2) % 2
        also = (lane // 32 == (row // 4) % 4) & ((lane // 16) % 2 == is_grad)
        m = [matches(e, k, also) for k in range(2)]
        scale = jnp.sum(m[0] * rw[0:1] + m[1] * rw[1:2], axis=1, keepdims=True)
        scale = jnp.where(is_grad[:, 0:1] == 1, scale, 1.0)
        picked = dot((m[0] + m[1]).astype(BF16), stacked(tok_cot[...], 4), 1, 0)
        send1[e] = (picked * scale).astype(BF16)

    first = {}

    def over_ex(e):
        first[e] = []
        for k in (6, 2, 5, 7, 4, 1, 3):
            part = pl.ds(k * TILE, TILE)
            first[e].append(remote(send1.at[e, part], recv1.at[e, part], peer(k, 1)))
        recv1[e, 0:TILE] = send1[e, 0:TILE]

    regroup = onehot(
        lane == ((row % 16) // 2) * 16 + (row // 32) * 4 + ((row // 16) % 2) * 2 + row % 2
    )

    def form(e):
        for copy in first[e]:
            copy.wait_recv()
        block = dot(regroup, recv1[e], 1, 0).astype(BF16)
        for q in range(4):
            cols = slice(q * quarter, (q + 1) * quarter)
            rows[2 * e, 0:TILE, cols] = block[q * 32 : q * 32 + 16]
            rows[2 * e + 1, 0:TILE, cols] = block[q * 32 + 16 : q * 32 + 32]

    arrive = {}

    def move(s, here, there, device):
        src = rows.at[s, pl.ds(block_row(*here), TILE)]
        dst = rows.at[s, pl.ds(block_row(*there), TILE)]
        arrive[s, there] = remote(src, dst, device)

    def share(s, dyl, dz):
        move(s, (0, dyl, dz), (1, dyl, dz), sibling)

    def arrived(s, *block):
        arrive[s, block].wait_recv()

    def around(s, dyl):
        move(s, (0, dyl, 0), (0, dyl, 3), z_plus)
        move(s, (0, dyl, 0), (0, dyl, 1), z_minus)
        move(s, (0, dyl, 0), (0, dyl, 2), z_far)

    def across(s, dz):
        move(s, (0, 0, dz), (0, 1, dz), y_pair)

    def pass_on(s, dyl, dz):
        arrived(s, 0, dyl, dz)
        share(s, dyl, dz)

    def pass_across(s, dz):
        arrived(s, 0, 0, dz)
        across(s, dz)
        share(s, 0, dz)

    def shared(s):
        for dyl in range(2):
            for dz in range(4):
                arrived(s, 1, dyl, dz)

    c0, c1 = 0.7978845608028654, 0.044715
    step = hidden // 2

    def forward_inputs(e, f):
        cols = pl.ds(f * step, step)
        pre[0, :, cols] = dot(rows[2 * e], wg[e, :, cols], 1, 0)
        pre[1, :, cols] = dot(rows[2 * e], wu[e, :, cols], 1, 0)

    def forward_grads(e, f):
        cols = pl.ds(f * step, step)
        grad_hidden = dot(rows[2 * e + 1], wd[e, cols, :], 1, 1)
        pre_gate, pre_up = pre[0, :, cols], pre[1, :, cols]
        square = pre_gate * pre_gate
        t = jnp.tanh(c0 * (pre_gate + c1 * (pre_gate * square)))
        cdf = 0.5 * (1.0 + t)
        act = pre_gate * cdf
        slope = cdf + (0.5 * c0) * pre_gate * (1.0 - t * t) * (1.0 + (3.0 * c1) * square)
        hid[e, :, cols] = (act * pre_up).astype(BF16)
        gu[e, :, cols] = (grad_hidden * act).astype(BF16)
        gg[e, :, cols] = (grad_hidden * pre_up * slope).astype(BF16)

    pair = {}

    def input_grad(e, d):
        cols = pl.ds(d * quarter, quarter)
        part = dot(gg[e], wg[e, cols, :], 1, 1) + dot(gu[e], wu[e, cols, :], 1, 1)
        pair_out[e, :, cols] = part[HALF_ROWS:].astype(BF16)
        acc[e, :, cols] = part[:HALF_ROWS]
        pair[e, d] = remote(pair_out.at[e, :, cols], pair_in.at[e, :, cols], sibling)

    def weight_grad(e, which):
        if which == 0:
            dgate_ref[e] = dot(rows[2 * e], gg[e], 0, 0).astype(BF16)
        elif which == 1:
            dup_ref[e] = dot(rows[2 * e], gu[e], 0, 0).astype(BF16)
        else:
            ddown_ref[e] = dot(hid[e], rows[2 * e + 1], 0, 0).astype(BF16)

    hop = {}

    def send_back(e, h):
        for d in (2 * h, 2 * h + 1):
            pair[e, d].wait_recv()
        cols = pl.ds(h * half, half)
        both = acc[e, :, cols] + pair_in[e, :, cols].astype(F32)
        acc[e, 0:TILE, cols] = both[0:TILE]
        back_out[e, TILE:, cols] = both[TILE:].astype(BF16)
        for b in (6, 5, 7, 2, 4, 1, 3):
            block = pl.ds(b * TILE, TILE)
            hop[e, h, b] = remote(
                back_out.at[e, block, cols], back_in.at[e, block, cols], mate(b)
            )

    ungroup = onehot(lane == ((row // 2) % 8) * 16 + (row // 16) * 2 + row % 2)

    def back_over_ex(e):
        for h in range(2):
            for b in range(1, 8):
                hop[e, h, b].wait_recv()
        summed = acc[e, 0:TILE]
        for b in range(1, 8):
            summed += back_in[e, b * TILE : (b + 1) * TILE].astype(F32)
        summed = summed.astype(BF16)
        ret_out[e] = dot(ungroup, stacked(summed, 8), 1, 0).astype(BF16)
        for k in (6, 2, 5, 7, 4, 1, 3):
            part = pl.ds(k * TILE, TILE)
            into = ret_in.at[pl.ds(e * 128 + k * TILE, TILE)]
            hop[e, k] = remote(ret_out.at[e, part], into, peer(k, -1))
        ret_in[e * 128 : e * 128 + TILE] = ret_out[e, 0:TILE]

    def combine():
        here = lane // 16 == (row // 2) % 8
        pick = jnp.concatenate(
            [(matches(e, 0, here) + matches(e, 1, here)).astype(BF16) for e in range(2)], axis=0
        )
        for e in range(2):
            for k in range(1, PEERS):
                hop[e, k].wait_recv()
        out = dot(pick, ret_in[...], 0, 0).astype(BF16)
        for q in range(8):
            gtok_ref[:, q * eighth : (q + 1) * eighth] = out[q * 16 : (q + 1) * 16]

    tok_load.wait()
    cot_load.wait()
    build(0)
    pl.semaphore_wait(barrier, len(partners))
    over_ex(0)
    build(1)
    over_ex(1)
    form(0)
    across(0, 0)
    around(1, 0)
    around(0, 0)
    across(1, 0)
    share(0, 0, 0)
    share(1, 0, 0)
    form(1)
    across(2, 0)
    around(3, 0)
    across(3, 0)
    share(2, 0, 0)
    share(3, 0, 0)
    arrived(0, 0, 1, 0)
    around(0, 1)
    share(0, 1, 0)
    around(2, 0)
    for dz in (3, 1, 2):
        pass_across(1, dz)
    for dz in (3, 1, 2):
        pass_on(0, 0, dz)
    pass_on(1, 1, 0)
    arrived(2, 0, 1, 0)
    around(2, 1)
    share(2, 1, 0)
    for dz in (3, 1, 2):
        pass_across(3, dz)
    for dz in (3, 1, 2):
        pass_on(0, 1, dz)
    for dz in (3, 1, 2):
        pass_on(1, 1, dz)
    shared(0)
    for n in range(3):
        weights[n].wait()
    forward_inputs(0, 0)
    forward_inputs(0, 1)
    for dz in (3, 1, 2):
        pass_on(2, 0, dz)
    pass_on(3, 1, 0)
    shared(1)
    forward_grads(0, 0)
    forward_grads(0, 1)
    for d in range(2):
        input_grad(0, d)
    for dz in (3, 1, 2):
        pass_on(2, 1, dz)
    for d in range(2, 4):
        input_grad(0, d)
    for dz in (3, 1, 2):
        pass_on(3, 1, dz)
    send_back(0, 0)
    send_back(0, 1)
    for n in range(3, 6):
        weights[n].wait()
    shared(2)
    forward_inputs(1, 0)
    forward_inputs(1, 1)
    shared(3)
    forward_grads(1, 0)
    forward_grads(1, 1)
    input_grad(1, 0)
    input_grad(1, 1)
    input_grad(1, 2)
    input_grad(1, 3)
    send_back(1, 0)
    send_back(1, 1)
    weight_grad(0, 0)
    back_over_ex(0)
    weight_grad(0, 1)
    weight_grad(0, 2)
    back_over_ex(1)
    weight_grad(1, 0)
    weight_grad(1, 1)
    weight_grad(1, 2)
    combine()
    for copy in sent:
        copy.wait_send()


def write_kernel(a_ref, b_ref, c_ref, d_ref, a_hbm, b_hbm, c_hbm, d_hbm, sem):
    copies = [
        pltpu.make_async_copy(src, dst, sem.at[n])
        for n, (src, dst) in enumerate(
            ((a_ref, a_hbm), (b_ref, b_hbm), (c_ref, c_hbm), (d_ref, d_hbm))
        )
    ]
    for copy in copies:
        copy.start()
    for copy in copies:
        copy.wait()


def per_device(tokens, cotangent, route_weights, expert_ids, slot_ids, gate, up, down):
    local, width, hidden = gate.shape
    count = tokens.shape[0]
    total = BLOCKS * TILE
    vmem = pl.BlockSpec(memory_space=pltpu.VMEM)
    hbm = pl.BlockSpec(memory_space=pltpu.HBM)
    results = pl.pallas_call(
        main_kernel,
        out_shape=(
            pltpu.VMEM((count, width), BF16),
            pltpu.VMEM((local, width, hidden), BF16),
            pltpu.VMEM((local, width, hidden), BF16),
            pltpu.VMEM((local, hidden, width), BF16),
        ),
        in_specs=[hbm] * 2 + [vmem] * 3 + [hbm] * 3,
        out_specs=[vmem] * 4,
        scratch_shapes=[
            pltpu.VMEM((2 * count, width), BF16),
            pltpu.VMEM((4, total, width), BF16),
            pltpu.VMEM((local, total, hidden), BF16),
            pltpu.VMEM((local, total, hidden), BF16),
            pltpu.VMEM((local, total, hidden), BF16),
            pltpu.VMEM((2, total, hidden), F32),
            pltpu.VMEM((local, width, hidden), BF16),
            pltpu.VMEM((local, width, hidden), BF16),
            pltpu.VMEM((local, hidden, width), BF16),
            pltpu.VMEM((2, 128, width // 4), BF16),
            pltpu.VMEM((2, 128, width // 4), BF16),
            pltpu.VMEM((2, HALF_ROWS, width), F32),
            pltpu.VMEM((2, HALF_ROWS, width), BF16),
            pltpu.VMEM((2, HALF_ROWS, width), BF16),
            pltpu.VMEM((2, HALF_ROWS, width), BF16),
            pltpu.VMEM((2, HALF_ROWS, width), BF16),
            pltpu.VMEM((2, 128, width // 8), BF16),
            pltpu.VMEM((256, width // 8), BF16),
            pltpu.SemaphoreType.DMA((8,)),
            pltpu.SemaphoreType.DMA((150,)),
            pltpu.SemaphoreType.DMA((150,)),
        ],
        compiler_params=pltpu.CompilerParams(
            collective_id=0, has_side_effects=True, vmem_limit_bytes=46 * 1024 * 1024
        ),
    )(tokens, cotangent, route_weights.T, expert_ids.T, slot_ids.T, gate, up, down)
    return pl.pallas_call(
        write_kernel,
        out_shape=tuple(jax.ShapeDtypeStruct(a.shape, BF16) for a in results),
        in_specs=[vmem] * 4,
        out_specs=[hbm] * 4,
        scratch_shapes=[pltpu.SemaphoreType.DMA((4,))],
        compiler_params=pltpu.CompilerParams(vmem_limit_bytes=4 * 1024 * 1024),
    )(*results)


def solution(mesh):
    return jax.shard_map(
        per_device,
        mesh=mesh,
        in_specs=(
            P(("ex", "ey", "dp"), None),
            P(("ex", "ey", "dp"), None),
            P(("ex", "ey", "dp"), None),
            P(("ex", "ey", "dp"), None),
            P(("ex", "ey", "dp"), None),
            P("ex", None, ("ey", "dp")),
            P("ex", None, ("ey", "dp")),
            P("ex", ("ey", "dp"), None),
        ),
        out_specs=(
            P(("ex", "ey", "dp"), None),
            P("ex", None, ("ey", "dp")),
            P("ex", None, ("ey", "dp")),
            P("ex", ("ey", "dp"), None),
        ),
        check_vma=False,
    )
```
